128 devices in a mesh: batch: 16 (over z_lo, y, core), rows: 8 (over z_hi, x).
Axes of the slice: x: 4, y: 4, z: 4 (z_hi: 2, z_lo: 2; z = z_hi * 2 + z_lo), core: 2. Of those that a mesh axis runs over, the one named last changes fastest.
Arguments:
- patches: bfloat16 [4096, 256, 256], P(('batch', 'rows')), parts along dimension 0, may hold values from -6 to 6
- conv_weight: float32 [49, 256], replicated, may hold values from -0.6 to 0.6
- conv_bias: float32 [256], replicated, may hold values from -2 to 2
- norm_gain: float32 [3, 256], replicated, may hold values from 0.1 to 1.9
- row_qkv: bfloat16 [256, 768], replicated, may hold values from -0.375 to 0.375
- row_out: bfloat16 [256, 256], replicated, may hold values from -0.375 to 0.375
- col_qkv: bfloat16 [256, 768], replicated, may hold values from -0.375 to 0.375
- col_out: bfloat16 [256, 256], replicated, may hold values from -0.375 to 0.375
- up_weight: bfloat16 [256, 1024], replicated, may hold values from -0.375 to 0.375
- down_weight: bfloat16 [1024, 256], replicated, may hold values from -0.1875 to 0.1875
Outputs:
- encoded: bfloat16 [4096, 256, 256], P(('batch', 'rows')), parts along dimension 0
The draws below stay inside these ranges and needn't reach their ends.
There are 16 independent parts, one for each index of `batch`. The reference program is written for one: setup_inputs(seed, part) draws one part's arguments, and reference() takes and returns one part's arrays. A program takes and returns all parts, laid end to end along the dimension named above; an argument that names none is the same for every part. Nothing has to cross between parts.
All inputs are finite; a program needn't handle non-finite values.
Results may differ from the reference program's by a relative error of at most 0.0095.
Values may be sent and summed in bfloat16 or wider, within the bound.
A program may use at most 128 MiB of HBM per device.

```python
import jax
import jax.numpy as jnp
from jax import lax

C = 256
HEADS = 8
FF = 1024
KS = 7
COLS = 256
ROWSP = 256


def level_of(key, shape, cuts, low, high):
    factor_of, own = 1.0, jax.random.fold_in(key, 6)
    for dim, shards_of in cuts:
        heights = jnp.exp(jax.random.uniform(jax.random.fold_in(own, dim), (shards_of,), jnp.float32, low / len(cuts), high / len(cuts)))
        factor_of = factor_of * jnp.repeat(heights, shape[dim] // shards_of).reshape([-1 if axis == dim else 1 for axis in range(len(shape))])
    return factor_of


def centred(own_key, shape, scale, reach, split=(), dtype=jnp.bfloat16):
    drawn = scale * jax.random.normal(own_key, shape, jnp.float32)
    if split:
        drawn = drawn * level_of(own_key, shape, split, -0.22, 0.18)
    return jnp.clip(drawn, -reach, reach).astype(dtype)


def setup_inputs(seed: int = 0, part: int = 0) -> dict:
    splits = jax.random.split(jax.random.key(seed), 11)
    part_keys = jax.random.split(jax.random.fold_in(splits[10], part), 11)
    return {
        "patches": centred(part_keys[0], (ROWSP, COLS, C), 1.0, 6.0, ((0, 8),)),
        "conv_weight": centred(splits[1], (KS * KS, C), 0.15, 0.6, (), jnp.float32),
        "conv_bias": centred(splits[2], (C,), 0.5, 2.0, (), jnp.float32),
        "norm_gain": jnp.clip(1.0 + 0.18 * jax.random.normal(splits[3], (3, C), jnp.float32), 0.1, 1.9),
        "row_qkv": centred(splits[4], (C, 3 * C), C ** -0.5, 0.375),
        "row_out": centred(splits[5], (C, C), C ** -0.5, 0.375),
        "col_qkv": centred(splits[6], (C, 3 * C), C ** -0.5, 0.375),
        "col_out": centred(splits[7], (C, C), C ** -0.5, 0.375),
        "up_weight": centred(splits[8], (C, FF), C ** -0.5, 0.375),
        "down_weight": centred(splits[9], (FF, C), FF ** -0.5, 0.1875),
    }


epsilon = 1e-05

def normalize(activation, scale_gain):
    activation = activation.astype(jnp.float32)
    center = activation - lax.optimization_barrier(jnp.mean(activation, axis=-1, keepdims=True))
    spread = lax.optimization_barrier(jnp.mean(center * center, axis=-1, keepdims=True))
    return (center * lax.rsqrt(spread + epsilon) * scale_gain).astype(jnp.bfloat16)

def attend(normed, w_qkv, w_out, head_count):
    channels = normed.shape[-1]
    head_size = channels // head_count
    projected = jnp.einsum('bsc,cd->bsd', normed.astype(jnp.float32), w_qkv.astype(jnp.float32)).astype(jnp.bfloat16)
    split_shape = normed.shape[:2] + (head_count, head_size)
    query_part = projected[..., :channels].reshape(split_shape).astype(jnp.float32)
    key_part = projected[..., channels:2 * channels].reshape(split_shape).astype(jnp.float32)
    value_part = projected[..., 2 * channels:].reshape(split_shape).astype(jnp.float32)
    scores = jnp.einsum('bqhd,bkhd->bhqk', query_part, key_part) * head_size ** (-0.5)
    attn_probs = jax.nn.softmax(scores, axis=-1).astype(jnp.bfloat16)
    context = jnp.einsum('bhqk,bkhd->bqhd', attn_probs.astype(jnp.float32), value_part).astype(jnp.bfloat16)
    context = context.reshape(normed.shape)
    return jnp.einsum('bsc,cd->bsd', context.astype(jnp.float32), w_out.astype(jnp.float32))

def depthwise(patches, conv_weight, conv_bias):
    margin = KS // 2
    row_count, col_count = (patches.shape[0], patches.shape[1])
    padded = jnp.pad(patches.astype(jnp.float32), ((margin, margin), (margin, margin), (0, 0)))
    summed = patches.astype(jnp.float32) + conv_bias
    for row_off in range(KS):
        for col_off in range(KS):
            summed = summed + padded[row_off:row_off + row_count, col_off:col_off + col_count] * conv_weight[row_off * KS + col_off]
    return summed.astype(jnp.bfloat16)

def reference(patches, conv_weight, conv_bias, norm_gain, row_qkv, row_out, col_qkv, col_out, up_weight, down_weight):
    convolved = depthwise(patches, conv_weight, conv_bias)
    normed = normalize(convolved, norm_gain[0])

    def row_pass(sequence):
        return attend(sequence[None], row_qkv, row_out, HEADS)[0]
    row_change = lax.map(row_pass, normed)
    after_rows = (convolved.astype(jnp.float32) + row_change).astype(jnp.bfloat16)
    normed = normalize(after_rows, norm_gain[1])

    def col_pass(sequence):
        return attend(sequence[None], col_qkv, col_out, HEADS)[0].astype(jnp.bfloat16)
    col_change = lax.map(col_pass, jnp.swapaxes(normed, 0, 1))
    after_cols = (after_rows.astype(jnp.float32) + jnp.swapaxes(col_change, 0, 1).astype(jnp.float32)).astype(jnp.bfloat16)
    normed = normalize(after_cols, norm_gain[2])

    def feed_forward(sequence):
        hidden = jax.nn.gelu(jnp.dot(sequence, up_weight, preferred_element_type=jnp.float32)).astype(jnp.bfloat16)
        return jnp.dot(hidden, down_weight, preferred_element_type=jnp.float32)
    mlp_change = lax.map(feed_forward, normed)
    return (after_cols.astype(jnp.float32) + mlp_change).astype(jnp.bfloat16)
```

```python
import functools
import math

import jax
import jax.numpy as jnp
from jax import lax
from jax.experimental import pallas as pl
from jax.experimental.pallas import tpu as pltpu
from jax.sharding import PartitionSpec as P

MESH = pl.DeviceIdType.MESH
f32, bf16 = jnp.float32, jnp.bfloat16
HEADS = 8
KS = 7
MARGIN = 3
C = 256
S = 256
N = 8
LOCAL = 32
TILE = 16
SCALE = math.log2(math.e) / math.sqrt(C // HEADS)

NN = (((1,), (0,)), ((), ()))
NT = (((1,), (1,)), ((), ()))
dot = functools.partial(lax.dot_general, preferred_element_type=f32)


def normalize(x, gain):
    center = x - jnp.mean(x, axis=-1, keepdims=True)
    spread = jnp.mean(center * center, axis=-1, keepdims=True)
    return (center * lax.rsqrt(spread + 1e-5) * gain).astype(bf16)


def attend(normed, w_qkv, w_key_t, w_out):
    query = (dot(normed, w_qkv[:, :C], NN) * SCALE).astype(bf16)
    value = dot(normed, w_qkv[:, 2 * C :], NN).astype(bf16)
    key_t = dot(w_key_t[...], normed, NT).astype(bf16)
    head_of = lax.broadcasted_iota(jnp.int32, (S, 128), 1) // 32
    zeros = jnp.zeros((32, S), bf16)
    ones = jnp.ones((S, 128), bf16)
    context = []
    for g in range(2):
        lanes = slice(128 * g, 128 * g + 128)
        value_g = jnp.concatenate([value[:, lanes], ones], axis=1)
        total = None
        for i in range(4):
            h = 4 * g + i
            key_h = jnp.concatenate(
                [key_t[32 * h : 32 * h + 32] if j == i else zeros for j in range(4)], axis=0
            )
            scores = dot(query[:, lanes], key_h, NN)
            top = jnp.max(scores, axis=1, keepdims=True)
            probs = jnp.exp2((scores - top).astype(bf16))
            both = dot(probs, value_g, NN)
            part = both[:, :128] * (1.0 / both[:, 128:])
            total = part if total is None else jnp.where(head_of == i, part, total)
        context.append(total.astype(bf16))
    return dot(jnp.concatenate(context, axis=1), w_out[...], NN)


def feed(normed, up, down):
    total = None
    for j in range(4):
        part = slice(256 * j, 256 * j + 256)
        hidden = jax.nn.gelu(dot(normed, up[:, part], NN)).astype(bf16)
        change = dot(hidden, down[part, :], NN)
        total = change if total is None else total + change
    return total


def convolve(xin, taps, bias, sums, r, store):
    for half in range(2):
        lanes = slice(128 * half, 128 * half + 128)
        for t in range(S // TILE + 1):
            if t < S // TILE:
                at = TILE * t
                rows = [
                    xin[r + a, at : at + TILE, lanes].astype(f32).reshape(TILE // 8, 8, 128)
                    for a in range(KS)
                ]
                for b in range(KS):
                    total = None
                    for a in range(KS):
                        term = rows[a] * taps[a * KS + b, :, lanes][None]
                        total = term if total is None else total + term
                    sums[half, b, 8 + at : 8 + at + TILE, :] = total.reshape(TILE, 128)
            if t:
                at = TILE * (t - 1)
                y = xin[r + MARGIN, at : at + TILE, lanes].astype(f32) + bias[:, lanes]
                for b in range(KS):
                    first = 8 + at + b - MARGIN
                    y = y + sums[half, b, first : first + TILE, :]
                store(at, lanes, y.astype(bf16))


def kernel(
    x_hbm, conv_w, bias, gains, row_qkv, row_out, col_qkv, col_out, up, down,
    out_hbm,
    xin, taps, sums, conv, row_kt, col_kt, swap, send1, recv1, cols, send2, recv2, outb,
    in_sem, halo_send, halo_recv, own1, send_sem1, recv_sem1, send_sem2, recv_sem2, out_sem,
):
    me = lax.axis_index("rows")
    last = N - 1

    load = pltpu.make_async_copy(x_hbm, xin.at[pl.ds(MARGIN, LOCAL)], in_sem)
    load.start()

    barrier = pltpu.get_barrier_semaphore()
    for i in range(1, N):
        pl.semaphore_signal(
            barrier, inc=1, device_id={"rows": lax.rem(me + i, N)}, device_id_type=MESH
        )
    pl.semaphore_wait(barrier, N - 1)

    def halo(which, target):
        first = LOCAL - MARGIN if which == 0 else 0
        put = 0 if which == 0 else MARGIN + LOCAL
        return pltpu.make_async_remote_copy(
            x_hbm.at[pl.ds(first, MARGIN)],
            xin.at[pl.ds(put, MARGIN)],
            halo_send.at[which],
            halo_recv.at[which],
            device_id={"rows": target},
            device_id_type=MESH,
        )

    @pl.when(me < last)
    def _():
        halo(0, lax.rem(me + 1, N)).start()

    @pl.when(me > 0)
    def _():
        halo(1, lax.rem(me + N - 1, N)).start()

    @pl.when(me == 0)
    def _():
        xin[0:MARGIN] = jnp.zeros((MARGIN, S, C), bf16)

    @pl.when(me == last)
    def _():
        xin[MARGIN + LOCAL :] = jnp.zeros((MARGIN, S, C), bf16)

    for t in range(KS * KS):
        taps[t] = jnp.broadcast_to(conv_w[t : t + 1, :], (8, C))
    sums[:, :, 0:8, :] = jnp.zeros((2, KS, 8, 128), f32)
    sums[:, :, 8 + S :, :] = jnp.zeros((2, KS, 8, 128), f32)
    row_kt[...] = row_qkv[:, C : 2 * C].T
    col_kt[...] = col_qkv[:, C : 2 * C].T
    i0 = lax.broadcasted_iota(jnp.int32, (256, 256), 0)
    i1 = lax.broadcasted_iota(jnp.int32, (256, 256), 1)
    swap[...] = jnp.where(
        (i0 // 16 == i1 % 16) & (i0 % 16 == i1 // 16), jnp.float32(1), jnp.float32(0)
    ).astype(bf16)

    load.wait()

    def row_step(p, _):
        @pl.when(p == (LOCAL - 2 * MARGIN) // 2)
        def _():
            @pl.when(me > 0)
            def _():
                halo(0, me).wait_recv()

            @pl.when(me < last)
            def _():
                halo(1, me).wait_recv()

        for u in range(2):
            slot = 2 * p + u
            r = lax.rem(slot + MARGIN, LOCAL)

            def store(at, lanes, y, u=u):
                conv[u, at : at + TILE, lanes] = y

            convolve(xin, taps, bias, sums, r, store)
        for u in range(2):
            x = conv[u].astype(f32)
            normed = normalize(x, gains[0:1, :])
            send1[2 * p + u] = (x + attend(normed, row_qkv, row_kt, row_out)).astype(bf16)
        half = p // 8
        at = lax.rem(p, 8) * 2
        for i in range(1, N):
            to = lax.rem(me + i, N)
            pltpu.make_async_remote_copy(
                send1.at[pl.ds(2 * p, 2), pl.ds(pl.multiple_of(to * LOCAL, LOCAL), LOCAL)],
                recv1.at[half, N - i, pl.ds(at, 2)],
                send_sem1,
                recv_sem1.at[half],
                device_id={"rows": to},
                device_id_type=MESH,
            ).start()
        pltpu.make_async_copy(
            send1.at[pl.ds(2 * p, 2), pl.ds(pl.multiple_of(me * LOCAL, LOCAL), LOCAL)],
            recv1.at[half, 0, pl.ds(at, 2)],
            own1.at[half],
        ).start()
        return 0

    lax.fori_loop(0, LOCAL // 2, row_step, 0)

    for half in range(2):
        pltpu.make_async_copy(recv1.at[half, 0], recv1.at[half, 0], own1.at[half]).wait()
        arrived = recv1.at[half, pl.ds(1, N - 1)]
        pltpu.make_async_copy(arrived, arrived, recv_sem1.at[half]).wait()

        def turn(j, _, half=half):
            for g in range(2):
                block = recv1[half, j, :, 16 * g : 16 * g + 16, :].reshape(256, C)
                turned = dot(swap[...], block, NN).astype(bf16).reshape(16, 16, C)
                cols[16 * g : 16 * g + 16, pl.ds(pl.multiple_of(j * 32 + 16 * half, 16), 16), :] = turned
            return 0

        lax.fori_loop(0, N, turn, 0)

    def col_step(p, _):
        half = p // 8
        at = lax.rem(p, 8) * 2
        for u in range(2):
            x = cols[2 * p + u].astype(f32)
            normed = normalize(x, gains[1:2, :])
            delta = attend(normed, col_qkv, col_kt, col_out).astype(bf16)
            y = (x + delta.astype(f32)).astype(bf16).astype(f32)
            normed = normalize(y, gains[2:3, :])
            z = (y + feed(normed, up, down)).astype(bf16)
            send2[2 * p + u] = z
            recv2[half, 0, at + u] = z[:LOCAL]
        for i in range(1, N):
            pltpu.make_async_remote_copy(
                send2.at[pl.ds(2 * p, 2), pl.ds(LOCAL * i, LOCAL)],
                recv2.at[half, N - i, pl.ds(at, 2)],
                send_sem2,
                recv_sem2.at[half],
                device_id={"rows": lax.rem(me + i, N)},
                device_id_type=MESH,
            ).start()
        return 0

    lax.fori_loop(0, LOCAL // 2, col_step, 0)

    for half in range(2):
        arrived = recv2.at[half, pl.ds(1, N - 1)]
        pltpu.make_async_copy(arrived, arrived, recv_sem2.at[half]).wait()

        def back(j, _, half=half):
            column = pl.multiple_of(lax.rem(me + j, N) * LOCAL + 16 * half, 16)
            for g in range(2):
                block = recv2[half, j, :, 16 * g : 16 * g + 16, :].reshape(256, C)
                turned = dot(swap[...], block, NN).astype(bf16).reshape(16, 16, C)
                first = 16 * g + MARGIN
                head = min(16, LOCAL - first)
                outb[first : first + head, pl.ds(column, 16), :] = turned[:head]
                if head < 16:
                    outb[0 : 16 - head, pl.ds(column, 16), :] = turned[head:]
            pltpu.make_async_copy(
                outb.at[:, pl.ds(column, 16)], out_hbm.at[:, pl.ds(column, 16)], out_sem
            ).start()
            return 0

        lax.fori_loop(0, N, back, 0)

    pltpu.make_async_copy(outb, out_hbm, out_sem).wait()
    sent = send1.at[pl.ds(0, LOCAL // N * (N - 1))]
    pltpu.make_async_copy(sent, sent, send_sem1).wait()
    sent = send2.at[pl.ds(0, LOCAL // N * (N - 1))]
    pltpu.make_async_copy(sent, sent, send_sem2).wait()

    @pl.when(me < last)
    def _():
        halo(0, me).wait_send()

    @pl.when(me > 0)
    def _():
        halo(1, me).wait_send()


def on_device(
    patches, conv_weight, conv_bias, norm_gain, row_qkv, row_out, col_qkv, col_out, up_weight, down_weight
):
    vmem = pl.BlockSpec(memory_space=pltpu.VMEM)
    hbm = pl.BlockSpec(memory_space=pl.ANY)
    dma = pltpu.SemaphoreType.DMA
    return pl.pallas_call(
        kernel,
        out_shape=jax.ShapeDtypeStruct(patches.shape, bf16),
        in_specs=[hbm] + [vmem] * 9,
        out_specs=hbm,
        scratch_shapes=[
            pltpu.VMEM((LOCAL + 2 * MARGIN, S, C), bf16),
            pltpu.VMEM((KS * KS, 8, C), f32),
            pltpu.VMEM((2, KS, S + 16, 128), f32),
            pltpu.VMEM((2, S, C), bf16),
            pltpu.VMEM((C, C), bf16),
            pltpu.VMEM((C, C), bf16),
            pltpu.VMEM((256, 256), bf16),
            pltpu.VMEM((LOCAL, S, C), bf16),
            pltpu.VMEM((2, N, 16, LOCAL, C), bf16),
            pltpu.VMEM((LOCAL, S, C), bf16),
            pltpu.VMEM((LOCAL, S, C), bf16),
            pltpu.VMEM((2, N, 16, LOCAL, C), bf16),
            pltpu.VMEM((LOCAL, S, C), bf16),
            dma, dma((2,)), dma((2,)), dma((2,)), dma, dma((2,)), dma, dma((2,)), dma,
        ],
        compiler_params=pltpu.CompilerParams(
            collective_id=0, has_side_effects=True, vmem_limit_bytes=60 * 2**20
        ),
        cost_estimate=pl.CostEstimate(
            flops=34_000_000_000, bytes_accessed=12_000_000, transcendentals=50_000_000
        ),
    )(
        patches, conv_weight, conv_bias.reshape(1, C), norm_gain, row_qkv, row_out, col_qkv, col_out,
        up_weight, down_weight,
    )


def solution(mesh):
    return jax.shard_map(
        on_device,
        mesh=mesh,
        in_specs=(P(("batch", "rows"), None, None), P(), P(), P(), P(), P(), P(), P(), P(), P()),
        out_specs=P(("batch", "rows"), None, None),
        check_vma=False,
    )
```

```python
import functools
import math

import jax
import jax.numpy as jnp
from jax import lax
from jax.experimental import pallas as pl
from jax.experimental.pallas import tpu as pltpu
from jax.sharding import PartitionSpec as P

MESH = pl.DeviceIdType.MESH
f32, bf16 = jnp.float32, jnp.bfloat16
HEADS = 8
KS = 7
MARGIN = 3
C = 256
S = 256
N = 8
LOCAL = 32
TILE = 32
GELU_A = math.sqrt(2 / math.pi)
SCALE = math.log2(math.e) / math.sqrt(C // HEADS)

NN = (((1,), (0,)), ((), ()))
NT = (((1,), (1,)), ((), ()))
dot = functools.partial(lax.dot_general, preferred_element_type=f32)


def normalize(x, gain):
    center = x - jnp.mean(x, axis=-1, keepdims=True)
    spread = jnp.mean(center * center, axis=-1, keepdims=True)
    return (center * lax.rsqrt(spread + 1e-5) * gain).astype(bf16)


def heads(query, key_t, value, tick):
    head_of = lax.broadcasted_iota(jnp.int32, (S, 128), 1) // 32
    zeros = jnp.zeros((32, S), bf16)
    none = jnp.zeros((S, 128), bf16)
    one = jnp.ones((S, 128), bf16)

    def score(h):
        g, i = divmod(h, 4)
        key_h = jnp.concatenate(
            [key_t[32 * h : 32 * h + 32] if j == i else zeros for j in range(4)], axis=0
        )
        return dot(query[:, 128 * g : 128 * g + 128], key_h, NN)

    context = []
    scores = score(0)
    for g in range(2):
        value_g = value[:, 128 * g : 128 * g + 128]
        total = None
        for i in range(4):
            h = 4 * g + i
            later = score(h + 1) if h < HEADS - 1 else None
            top = jnp.max(scores, axis=1, keepdims=True)
            probs = jnp.exp2((scores - top).astype(bf16))
            tick(h)
            value_h = jnp.concatenate(
                [jnp.where(head_of == i, value_g, none), jnp.where(head_of == i, one, none)], axis=1
            )
            both = dot(probs, value_h, NN)
            total = both if total is None else total + both
            scores = later
        context.append((total[:, :128] / total[:, 128:]).astype(bf16))
    return jnp.concatenate(context, axis=1)


def gelu(x):
    half = 0.5 * x
    inner = x * (GELU_A + (GELU_A * 0.044715) * (x * x))
    return half + half * jnp.tanh(inner)


def tree_sum(terms):
    while len(terms) > 1:
        odd = [terms[-1]] if len(terms) % 2 else []
        terms = [a + b for a, b in zip(terms[::2], terms[1::2])] + odd
    return terms[0]


def convolve(xin, taps, bias, sums, r, store):
    for t in range(S // TILE + 1):
        if t < S // TILE:
            at = TILE * t
            rows = [xin[r + a, at : at + TILE, :] for a in range(KS)]
            for b in range(KS):
                total = tree_sum([rows[a] * taps[a * KS + b] for a in range(KS)]).astype(f32)
                for half in range(2):
                    sums[half, b, 8 + at : 8 + at + TILE, :] = total[:, 128 * half : 128 * half + 128]
        if t:
            at = TILE * (t - 1)
            y = xin[r + MARGIN, at : at + TILE, :].astype(f32) + bias[...]
            parts = []
            for half in range(2):
                part = y[:, 128 * half : 128 * half + 128]
                for b in range(KS):
                    first = 8 + at + b - MARGIN
                    part = part + sums[half, b, first : first + TILE, :]
                parts.append(part)
            store(at, jnp.concatenate(parts, axis=1).astype(bf16))
        yield


def kernel(
    x_hbm, conv_w, bias, gains, row_qkv, row_out, col_qkv, col_out, up, down,
    out_hbm,
    xin, taps, sums, query, key_t, value, context, row_kt, col_kt, swap, send1, recv1, cols, send2, recv2, outb,
    in_sem, halo_send, halo_recv, own1, own2, send_sem1, recv_sem1, send_sem2, recv_sem2, out_sem,
):
    me = lax.axis_index("rows")
    last = N - 1

    load = pltpu.make_async_copy(x_hbm, xin.at[pl.ds(MARGIN, LOCAL)], in_sem)
    load.start()

    barrier = pltpu.get_barrier_semaphore()
    for i in range(1, N):
        pl.semaphore_signal(
            barrier, inc=1, device_id={"rows": lax.rem(me + i, N)}, device_id_type=MESH
        )
    pl.semaphore_wait(barrier, N - 1)

    def halo(which, target):
        first = LOCAL - MARGIN if which == 0 else 0
        put = 0 if which == 0 else MARGIN + LOCAL
        return pltpu.make_async_remote_copy(
            x_hbm.at[pl.ds(first, MARGIN)],
            xin.at[pl.ds(put, MARGIN)],
            halo_send.at[which],
            halo_recv.at[which],
            device_id={"rows": target},
            device_id_type=MESH,
        )

    @pl.when(me < last)
    def _():
        halo(0, lax.rem(me + 1, N)).start()

    @pl.when(me > 0)
    def _():
        halo(1, lax.rem(me + N - 1, N)).start()

    @pl.when(me == 0)
    def _():
        xin[0:MARGIN] = jnp.zeros((MARGIN, S, C), bf16)

    @pl.when(me == last)
    def _():
        xin[MARGIN + LOCAL :] = jnp.zeros((MARGIN, S, C), bf16)

    for t in range(KS * KS):
        taps[t] = jnp.broadcast_to(conv_w[t : t + 1, :], (TILE, C)).astype(bf16)
    sums[:, :, 0:8, :] = jnp.zeros((2, KS, 8, 128), f32)
    sums[:, :, 8 + S :, :] = jnp.zeros((2, KS, 8, 128), f32)
    row_kt[...] = row_qkv[:, C : 2 * C].T
    col_kt[...] = col_qkv[:, C : 2 * C].T
    i0 = lax.broadcasted_iota(jnp.int32, (256, 256), 0)
    i1 = lax.broadcasted_iota(jnp.int32, (256, 256), 1)
    swap[...] = jnp.where(
        (i0 // 16 == i1 % 16) & (i0 % 16 == i1 // 16), jnp.float32(1), jnp.float32(0)
    ).astype(bf16)

    load.wait()

    def project(normed, w_qkv, w_key_t, s, part):
        if part == 0:
            query[s] = (dot(normed, w_qkv[:, :C], NN) * SCALE).astype(bf16)
        if part == 1:
            value[s] = dot(normed, w_qkv[:, 2 * C :], NN).astype(bf16)
        if part == 2:
            key_t[s] = dot(w_key_t[...], normed, NT).astype(bf16)

    def conv_slot(slot):
        def store(at, y):
            send1[slot + 1, at : at + TILE, :] = y

        return convolve(xin, taps, bias, sums, lax.rem(slot + MARGIN, LOCAL), store)

    def send_row(slot):
        half, at = slot // 16, lax.rem(slot, 16)
        for i in range(1, N):
            to = lax.rem(me + i, N)
            pltpu.make_async_remote_copy(
                send1.at[slot + 1, pl.ds(pl.multiple_of(to * LOCAL, LOCAL), LOCAL)],
                recv1.at[half, N - i, at],
                send_sem1,
                recv_sem1.at[half],
                device_id={"rows": to},
                device_id_type=MESH,
            ).start()
        pltpu.make_async_copy(
            send1.at[slot + 1, pl.ds(pl.multiple_of(me * LOCAL, LOCAL), LOCAL)],
            recv1.at[half, 0, at],
            own1.at[half],
        ).start()

    def first_conv(slot, _):
        for _ in conv_slot(slot):
            pass
        return 0

    lax.fori_loop(0, 2, first_conv, 0)
    normed = normalize(send1[1].astype(f32), gains[0:1, :])
    for part in range(3):
        project(normed, row_qkv, row_kt, 0, part)
    send1[0] = jnp.zeros((S, C), bf16)
    context[1] = jnp.zeros((S, C), bf16)

    def row_step(j, _):
        @pl.when(j == (LOCAL - 2 * MARGIN) // 2 - 1)
        def _():
            @pl.when(me > 0)
            def _():
                halo(0, me).wait_recv()

            @pl.when(me < last)
            def _():
                halo(1, me).wait_recv()

        for u in range(2):
            t = 2 * j + u
            pieces = conv_slot(t + 2)
            held = {}

            def tick(h, t=t, u=u, pieces=pieces, held=held):
                if h == 0:
                    held["normed"] = normalize(send1[t + 2].astype(f32), gains[0:1, :])
                if h == 2:
                    project(held["normed"], row_qkv, row_kt, 1 - u, 0)
                if h == 4:
                    project(held["normed"], row_qkv, row_kt, 1 - u, 1)
                if h == 5:
                    project(held["normed"], row_qkv, row_kt, 1 - u, 2)
                if h == 6:
                    change = dot(context[1 - u], row_out[...], NN)
                    send1[t] = (send1[t].astype(f32) + change).astype(bf16)

            context[u] = heads(query[u], key_t[u], value[u], tick)
            for _ in pieces:
                pass

        @pl.when(j > 0)
        def _():
            send_row(2 * j - 1)

        send_row(2 * j)
        return 0

    lax.fori_loop(0, LOCAL // 2, row_step, 0)
    send1[LOCAL] = (send1[LOCAL].astype(f32) + dot(context[1], row_out[...], NN)).astype(bf16)
    send_row(LOCAL - 1)

    for half in range(2):
        pltpu.make_async_copy(recv1.at[half, 0], recv1.at[half, 0], own1.at[half]).wait()
        arrived = recv1.at[half, pl.ds(1, N - 1)]
        pltpu.make_async_copy(arrived, arrived, recv_sem1.at[half]).wait()

        def turn(j, _, half=half):
            for g in range(2):
                block = recv1[half, j, :, 16 * g : 16 * g + 16, :].reshape(256, C)
                turned = dot(swap[...], block, NN).astype(bf16).reshape(16, 16, C)
                cols[16 * g : 16 * g + 16, pl.ds(pl.multiple_of(j * 32 + 16 * half, 16), 16), :] = turned
            return 0

        lax.fori_loop(0, N, turn, 0)

    def send_col(c):
        half, at = c // 16, lax.rem(c, 16)
        for i in range(1, N):
            pltpu.make_async_remote_copy(
                send2.at[c + 1, pl.ds(LOCAL * i, LOCAL)],
                recv2.at[half, N - i, at],
                send_sem2,
                recv_sem2.at[half],
                device_id={"rows": lax.rem(me + i, N)},
                device_id_type=MESH,
            ).start()
        pltpu.make_async_copy(send2.at[c + 1, pl.ds(0, LOCAL)], recv2.at[half, 0, at], own2.at[half]).start()

    def finish(held, s, c, part):
        if part == 0:
            delta = dot(context[s], col_out[...], NN).astype(bf16).astype(f32)
            y = (cols[c].astype(f32) + delta).astype(bf16)
            cols[c] = y
            held["inner"] = normalize(y.astype(f32), gains[2:3, :])
            return
        units = slice(256 * (part - 1), 256 * part)
        hidden = gelu(dot(held["inner"], up[:, units], NN)).astype(bf16)
        change = dot(hidden, down[units, :], NN)
        held["total"] = change if part == 1 else held["total"] + change
        if part == 4:
            send2[c + 1] = (cols[c].astype(f32) + held["total"]).astype(bf16)

    normed = normalize(cols[0].astype(f32), gains[1:2, :])
    for part in range(3):
        project(normed, col_qkv, col_kt, 0, part)
    context[1] = jnp.zeros((S, C), bf16)

    def col_step(j, _):
        for u in range(2):
            t = 2 * j + u
            held = {}

            def tick(h, t=t, u=u, held=held):
                if h == 0:
                    held["normed"] = normalize(
                        cols[jnp.minimum(t + 1, LOCAL - 1)].astype(f32), gains[1:2, :]
                    )
                if h == 1:
                    finish(held, 1 - u, t - 1 if u else jnp.maximum(t - 1, 0), 0)
                if h == 2:
                    project(held["normed"], col_qkv, col_kt, 1 - u, 0)
                if h == 3:
                    finish(held, 1 - u, t - 1 if u else jnp.maximum(t - 1, 0), 1)
                if h == 4:
                    project(held["normed"], col_qkv, col_kt, 1 - u, 1)
                    finish(held, 1 - u, t - 1 if u else jnp.maximum(t - 1, 0), 2)
                if h == 5:
                    project(held["normed"], col_qkv, col_kt, 1 - u, 2)
                    finish(held, 1 - u, t - 1 if u else jnp.maximum(t - 1, 0), 3)
                if h == 6:
                    finish(held, 1 - u, t - 1 if u else jnp.maximum(t - 1, 0), 4)

            context[u] = heads(query[u], key_t[u], value[u], tick)

        @pl.when(j > 0)
        def _():
            send_col(2 * j - 1)

        send_col(2 * j)
        return 0

    lax.fori_loop(0, LOCAL // 2, col_step, 0)
    held = {}
    for part in range(5):
        finish(held, 1, LOCAL - 1, part)
    send_col(LOCAL - 1)

    for half in range(2):
        pltpu.make_async_copy(recv2.at[half, 0], recv2.at[half, 0], own2.at[half]).wait()
        arrived = recv2.at[half, pl.ds(1, N - 1)]
        pltpu.make_async_copy(arrived, arrived, recv_sem2.at[half]).wait()

        def back(j, _, half=half):
            column = pl.multiple_of(lax.rem(me + j, N) * LOCAL + 16 * half, 16)
            for g in range(2):
                block = recv2[half, j, :, 16 * g : 16 * g + 16, :].reshape(256, C)
                turned = dot(swap[...], block, NN).astype(bf16).reshape(16, 16, C)
                first = 16 * g + MARGIN
                head = min(16, LOCAL - first)
                outb[first : first + head, pl.ds(column, 16), :] = turned[:head]
                if head < 16:
                    outb[0 : 16 - head, pl.ds(column, 16), :] = turned[head:]
            pltpu.make_async_copy(
                outb.at[:, pl.ds(column, 16)], out_hbm.at[:, pl.ds(column, 16)], out_sem
            ).start()
            return 0

        lax.fori_loop(0, N, back, 0)

    pltpu.make_async_copy(outb, out_hbm, out_sem).wait()
    sent = send1.at[pl.ds(0, LOCAL // N * (N - 1))]
    pltpu.make_async_copy(sent, sent, send_sem1).wait()
    sent = send2.at[pl.ds(0, LOCAL // N * (N - 1))]
    pltpu.make_async_copy(sent, sent, send_sem2).wait()

    @pl.when(me < last)
    def _():
        halo(0, me).wait_send()

    @pl.when(me > 0)
    def _():
        halo(1, me).wait_send()


def on_device(
    patches, conv_weight, conv_bias, norm_gain, row_qkv, row_out, col_qkv, col_out, up_weight, down_weight
):
    vmem = pl.BlockSpec(memory_space=pltpu.VMEM)
    hbm = pl.BlockSpec(memory_space=pl.ANY)
    dma = pltpu.SemaphoreType.DMA
    return pl.pallas_call(
        kernel,
        out_shape=jax.ShapeDtypeStruct(patches.shape, bf16),
        in_specs=[hbm] + [vmem] * 9,
        out_specs=hbm,
        scratch_shapes=[
            pltpu.VMEM((LOCAL + 2 * MARGIN, S, C), bf16),
            pltpu.VMEM((KS * KS, TILE, C), bf16),
            pltpu.VMEM((2, KS, S + 16, 128), f32),
            pltpu.VMEM((2, S, C), bf16),
            pltpu.VMEM((2, C, S), bf16),
            pltpu.VMEM((2, S, C), bf16),
            pltpu.VMEM((2, S, C), bf16),
            pltpu.VMEM((C, C), bf16),
            pltpu.VMEM((C, C), bf16),
            pltpu.VMEM((256, 256), bf16),
            pltpu.VMEM((LOCAL + 3, S, C), bf16),
            pltpu.VMEM((2, N, 16, LOCAL, C), bf16),
            pltpu.VMEM((LOCAL, S, C), bf16),
            pltpu.VMEM((LOCAL + 1, S, C), bf16),
            pltpu.VMEM((2, N, 16, LOCAL, C), bf16),
            pltpu.VMEM((LOCAL, S, C), bf16),
            dma, dma((2,)), dma((2,)), dma((2,)), dma((2,)), dma, dma((2,)), dma, dma((2,)), dma,
        ],
        compiler_params=pltpu.CompilerParams(
            collective_id=0, has_side_effects=True, vmem_limit_bytes=60 * 2**20
        ),
        cost_estimate=pl.CostEstimate(
            flops=34_000_000_000, bytes_accessed=12_000_000, transcendentals=50_000_000
        ),
    )(
        patches, conv_weight, conv_bias.reshape(1, C), norm_gain, row_qkv, row_out, col_qkv, col_out,
        up_weight, down_weight,
    )


def solution(mesh):
    return jax.shard_map(
        on_device,
        mesh=mesh,
        in_specs=(P(("batch", "rows"), None, None), P(), P(), P(), P(), P(), P(), P(), P(), P()),
        out_specs=P(("batch", "rows"), None, None),
        check_vma=False,
    )
```

```python
import functools
import math

import jax
import jax.numpy as jnp
from jax import lax
from jax.experimental import pallas as pl
from jax.experimental.pallas import tpu as pltpu
from jax.sharding import PartitionSpec as P

MESH = pl.DeviceIdType.MESH
f32, bf16 = jnp.float32, jnp.bfloat16
HEADS = 8
KS = 7
MARGIN = 3
C = 256
S = 256
N = 8
LOCAL = 32
TILE = 8
SOURCES = 2
GELU_A = math.sqrt(2 / math.pi)
SCALE = math.log2(math.e) / math.sqrt(C // HEADS)

NN = (((1,), (0,)), ((), ()))
NT = (((1,), (1,)), ((), ()))
dot = functools.partial(lax.dot_general, preferred_element_type=f32)


def normalize(x, gain):
    center = x - jnp.mean(x, axis=-1, keepdims=True)
    spread = jnp.mean(center * center, axis=-1, keepdims=True)
    return (center * lax.rsqrt(spread + 1e-5) * gain).astype(bf16)


def heads(query, key_t, value, tick, look=2):
    head_of = lax.broadcasted_iota(jnp.int32, (S, 128), 1) // 32
    zeros = jnp.zeros((32, S), bf16)
    none = jnp.zeros((S, 128), bf16)
    one = jnp.ones((S, 128), bf16)

    def score(h):
        g, i = divmod(h, 4)
        key_h = jnp.concatenate(
            [key_t[32 * h : 32 * h + 32] if j == i else zeros for j in range(4)], axis=0
        )
        return dot(query[:, 128 * g : 128 * g + 128], key_h, NN)

    context = []
    ahead = [score(h) for h in range(look)]
    for g in range(2):
        value_g = value[:, 128 * g : 128 * g + 128]
        total = None
        for i in range(4):
            h = 4 * g + i
            scores = ahead.pop(0)
            if h < HEADS - look:
                ahead.append(score(h + look))
            top = jnp.max(scores, axis=1, keepdims=True)
            probs = jnp.exp2((scores - top).astype(bf16))
            tick(h)
            value_h = jnp.concatenate(
                [jnp.where(head_of == i, value_g, none), jnp.where(head_of == i, one, none)], axis=1
            )
            both = dot(probs, value_h, NN)
            total = both if total is None else total + both
        context.append((total[:, :128] / total[:, 128:]).astype(bf16))
    return jnp.concatenate(context, axis=1)


def gelu(x):
    half = 0.5 * x
    inner = x * (GELU_A + (GELU_A * 0.044715) * (x * x))
    return half + half * jnp.tanh(inner)


def tree_sum(terms):
    while len(terms) > 1:
        odd = [terms[-1]] if len(terms) % 2 else []
        terms = [a + b for a, b in zip(terms[::2], terms[1::2])] + odd
    return terms[0]


def convolve(xin, taps, bias, sums, r, store):
    for t in range(S // TILE + 1):
        if t < S // TILE:
            at = TILE * t
            rows = [xin[r + a, at : at + TILE, :] for a in range(KS)]
            for b in range(KS):
                total = tree_sum([rows[a] * taps[a * KS + b] for a in range(KS)]).astype(f32)
                for half in range(2):
                    sums[half, b, 8 + at : 8 + at + TILE, :] = total[:, 128 * half : 128 * half + 128]
        if t:
            at = TILE * (t - 1)
            y = xin[r + MARGIN, at : at + TILE, :].astype(f32) + bias[...]
            parts = []
            for half in range(2):
                part = y[:, 128 * half : 128 * half + 128]
                for b in range(KS):
                    first = 8 + at + b - MARGIN
                    part = part + sums[half, b, first : first + TILE, :]
                parts.append(part)
            store(at, jnp.concatenate(parts, axis=1).astype(bf16))
        yield


ORDER = {
    0: [("finish", 0)],
    7: [
        ("finish", 1), ("finish", 2), ("norm", 0), ("finish", 3), ("finish", 4),
        ("project", 0), ("project", 1), ("project", 2),
    ],
}


def swap_matrix():
    i0 = lax.broadcasted_iota(jnp.int32, (256, 256), 0)
    i1 = lax.broadcasted_iota(jnp.int32, (256, 256), 1)
    chosen = (i0 // 16 == i1 % 16) & (i0 % 16 == i1 // 16)
    return jnp.where(chosen, jnp.float32(1), jnp.float32(0)).astype(bf16)


def rows_of_columns(landed, out, swap):
    @pl.when(pl.program_id(0) == 0)
    def _():
        swap[...] = swap_matrix()

    for source in range(SOURCES):
        for half in range(2):
            column = source * LOCAL + 16 * half
            for g in range(2):
                block = landed[source, 16 * half : 16 * half + 16, 16 * g : 16 * g + 16, :].reshape(256, C)
                turned = dot(swap[...], block, NN).astype(bf16).reshape(16, 16, C)
                first = 16 * g + MARGIN
                head = min(16, LOCAL - first)
                out[first : first + head, column : column + 16, :] = turned[:head]
                if head < 16:
                    out[0 : 16 - head, column : column + 16, :] = turned[head:]


def kernel(
    x_hbm, conv_w, bias, gains, row_qkv, row_out, col_qkv, col_out, up, down,
    landed,
    xin, taps, sums, query, key_t, value, context, row_kt, col_kt, swap, send1, recv1, cols, send2,
    in_sem, halo_send, halo_recv, own1, send_sem1, recv_sem1, send_sem2, recv_sem2,
):
    me = lax.axis_index("rows")
    last = N - 1

    load = pltpu.make_async_copy(x_hbm, xin.at[pl.ds(MARGIN, LOCAL)], in_sem)
    load.start()

    barrier = pltpu.get_barrier_semaphore()
    for i in range(1, N):
        pl.semaphore_signal(
            barrier, inc=1, device_id={"rows": lax.rem(me + i, N)}, device_id_type=MESH
        )
    def halo(which, target):
        first = LOCAL - MARGIN if which == 0 else 0
        put = 0 if which == 0 else MARGIN + LOCAL
        return pltpu.make_async_remote_copy(
            x_hbm.at[pl.ds(first, MARGIN)],
            xin.at[pl.ds(put, MARGIN)],
            halo_send.at[which],
            halo_recv.at[which],
            device_id={"rows": target},
            device_id_type=MESH,
        )

    @pl.when(me == 0)
    def _():
        xin[0:MARGIN] = jnp.zeros((MARGIN, S, C), bf16)

    @pl.when(me == last)
    def _():
        xin[MARGIN + LOCAL :] = jnp.zeros((MARGIN, S, C), bf16)

    for t in range(KS * KS):
        taps[t] = jnp.broadcast_to(conv_w[t : t + 1, :], (TILE, C)).astype(bf16)
    sums[:, :, 0:8, :] = jnp.zeros((2, KS, 8, 128), f32)
    sums[:, :, 8 + S :, :] = jnp.zeros((2, KS, 8, 128), f32)
    row_kt[...] = row_qkv[:, C : 2 * C].T
    col_kt[...] = col_qkv[:, C : 2 * C].T
    swap[...] = swap_matrix()

    load.wait()

    def project(normed, w_qkv, w_key_t, s, part):
        if part == 0:
            query[s] = (dot(normed, w_qkv[:, :C], NN) * SCALE).astype(bf16)
        if part == 1:
            value[s] = dot(normed, w_qkv[:, 2 * C :], NN).astype(bf16)
        if part == 2:
            key_t[s] = dot(w_key_t[...], normed, NT).astype(bf16)

    def conv_slot(slot):
        def store(at, y):
            send1[slot + 1, at : at + TILE, :] = y

        return convolve(xin, taps, bias, sums, lax.rem(slot + MARGIN, LOCAL), store)

    def send_rows(pair):
        half, at = pair // 8, 2 * lax.rem(pair, 8)
        slots = pl.ds(2 * pair + 1, 2)
        for i in range(1, N):
            to = lax.rem(me + i, N)
            pltpu.make_async_remote_copy(
                send1.at[slots, pl.ds(pl.multiple_of(to * LOCAL, LOCAL), LOCAL)],
                recv1.at[half, N - i, pl.ds(at, 2)],
                send_sem1,
                recv_sem1.at[half],
                device_id={"rows": to},
                device_id_type=MESH,
            ).start()
        pltpu.make_async_copy(
            send1.at[slots, pl.ds(pl.multiple_of(me * LOCAL, LOCAL), LOCAL)],
            recv1.at[half, 0, pl.ds(at, 2)],
            own1.at[half],
        ).start()

    def first_conv(slot, _):
        for _ in conv_slot(slot):
            pass
        return 0

    lax.fori_loop(0, 2, first_conv, 0)

    pl.semaphore_wait(barrier, N - 1)

    @pl.when(me < last)
    def _():
        halo(0, lax.rem(me + 1, N)).start()

    @pl.when(me > 0)
    def _():
        halo(1, lax.rem(me + N - 1, N)).start()

    normed = normalize(send1[1].astype(f32), gains[0:1, :])
    for part in range(3):
        project(normed, row_qkv, row_kt, 0, part)
    send1[0] = jnp.zeros((S, C), bf16)
    context[1] = jnp.zeros((S, C), bf16)

    def row_step(j, _):
        @pl.when(j == (LOCAL - 2 * MARGIN) // 2 - 1)
        def _():
            @pl.when(me > 0)
            def _():
                halo(0, me).wait_recv()

            @pl.when(me < last)
            def _():
                halo(1, me).wait_recv()

        for u in range(2):
            t = 2 * j + u
            pieces = conv_slot(t + 2)
            held = {}

            def tick(h, t=t, u=u, pieces=pieces, held=held):
                if h == 0:
                    held["normed"] = normalize(send1[t + 2].astype(f32), gains[0:1, :])
                if h == 2:
                    project(held["normed"], row_qkv, row_kt, 1 - u, 0)
                if h == 4:
                    project(held["normed"], row_qkv, row_kt, 1 - u, 1)
                if h == 5:
                    project(held["normed"], row_qkv, row_kt, 1 - u, 2)
                if h == 6:
                    change = dot(context[1 - u], row_out[...], NN)
                    send1[t] = (send1[t].astype(f32) + change).astype(bf16)

            context[u] = heads(query[u], key_t[u], value[u], tick)
            for _ in pieces:
                pass

        @pl.when(j > 0)
        def _():
            send_rows(j - 1)

        return 0

    lax.fori_loop(0, LOCAL // 2, row_step, 0)
    send1[LOCAL] = (send1[LOCAL].astype(f32) + dot(context[1], row_out[...], NN)).astype(bf16)
    send_rows(LOCAL // 2 - 1)

    for half in range(2):
        pltpu.make_async_copy(recv1.at[half, 0], recv1.at[half, 0], own1.at[half]).wait()
        arrived = recv1.at[half, pl.ds(1, N - 1)]
        pltpu.make_async_copy(arrived, arrived, recv_sem1.at[half]).wait()

        def turn(j, _, half=half):
            for g in range(2):
                block = recv1[half, j, :, 16 * g : 16 * g + 16, :].reshape(256, C)
                turned = dot(swap[...], block, NN).astype(bf16).reshape(16, 16, C)
                cols[16 * g : 16 * g + 16, pl.ds(pl.multiple_of(j * 32 + 16 * half, 16), 16), :] = turned
            return 0

        lax.fori_loop(0, N, turn, 0)

    def send_cols(pair):
        columns = pl.ds(2 * pair + 1, 2)
        for i in range(1, N):
            pltpu.make_async_remote_copy(
                send2.at[columns, pl.ds(LOCAL * i, LOCAL)],
                landed.at[me, pl.ds(2 * pair, 2)],
                send_sem2,
                recv_sem2,
                device_id={"rows": lax.rem(me + i, N)},
                device_id_type=MESH,
            ).start()
        pltpu.make_async_copy(
            send2.at[columns, pl.ds(0, LOCAL)], landed.at[me, pl.ds(2 * pair, 2)], recv_sem2
        ).start()

    def finish(held, s, c, part):
        if part == 0:
            delta = dot(context[s], col_out[...], NN).astype(bf16).astype(f32)
            y = (cols[c].astype(f32) + delta).astype(bf16)
            cols[c] = y
            held["inner"] = normalize(y.astype(f32), gains[2:3, :])
            return
        units = slice(256 * (part - 1), 256 * part)
        hidden = gelu(dot(held["inner"], up[:, units], NN)).astype(bf16)
        change = dot(hidden, down[units, :], NN)
        held["total"] = change if part == 1 else held["total"] + change
        if part == 4:
            send2[c + 1] = (cols[c].astype(f32) + held["total"]).astype(bf16)

    normed = normalize(cols[0].astype(f32), gains[1:2, :])
    for part in range(3):
        project(normed, col_qkv, col_kt, 0, part)
    context[1] = jnp.zeros((S, C), bf16)

    def col_step(j, _):
        for u in range(2):
            t = 2 * j + u
            held = {}

            def tick(h, t=t, u=u, held=held):
                before = t - 1 if u else jnp.maximum(t - 1, 0)
                for what, n in ORDER.get(h, ()):
                    if what == "norm":
                        held["normed"] = normalize(
                            cols[jnp.minimum(t + 1, LOCAL - 1)].astype(f32), gains[1:2, :]
                        )
                    if what == "project":
                        project(held["normed"], col_qkv, col_kt, 1 - u, n)
                    if what == "finish":
                        finish(held, 1 - u, before, n)

            context[u] = heads(query[u], key_t[u], value[u], tick, 3)

        @pl.when(j > 0)
        def _():
            send_cols(j - 1)

        return 0

    lax.fori_loop(0, LOCAL // 2, col_step, 0)
    held = {}
    for part in range(5):
        finish(held, 1, LOCAL - 1, part)
    send_cols(LOCAL // 2 - 1)

    pltpu.make_async_copy(landed, landed, recv_sem2).wait()
    sent = send1.at[pl.ds(0, LOCAL // N * (N - 1))]
    pltpu.make_async_copy(sent, sent, send_sem1).wait()
    sent = send2.at[pl.ds(0, LOCAL // N * (N - 1))]
    pltpu.make_async_copy(sent, sent, send_sem2).wait()

    @pl.when(me < last)
    def _():
        halo(0, me).wait_send()

    @pl.when(me > 0)
    def _():
        halo(1, me).wait_send()


def on_device(
    patches, conv_weight, conv_bias, norm_gain, row_qkv, row_out, col_qkv, col_out, up_weight, down_weight
):
    vmem = pl.BlockSpec(memory_space=pltpu.VMEM)
    hbm = pl.BlockSpec(memory_space=pl.ANY)
    dma = pltpu.SemaphoreType.DMA
    landed = pl.pallas_call(
        kernel,
        out_shape=jax.ShapeDtypeStruct((N, LOCAL, LOCAL, C), bf16),
        in_specs=[hbm] + [vmem] * 9,
        out_specs=hbm,
        scratch_shapes=[
            pltpu.VMEM((LOCAL + 2 * MARGIN, S, C), bf16),
            pltpu.VMEM((KS * KS, TILE, C), bf16),
            pltpu.VMEM((2, KS, S + 16, 128), f32),
            pltpu.VMEM((2, S, C), bf16),
            pltpu.VMEM((2, C, S), bf16),
            pltpu.VMEM((2, S, C), bf16),
            pltpu.VMEM((2, S, C), bf16),
            pltpu.VMEM((C, C), bf16),
            pltpu.VMEM((C, C), bf16),
            pltpu.VMEM((256, 256), bf16),
            pltpu.VMEM((LOCAL + 3, S, C), bf16),
            pltpu.VMEM((2, N, 16, LOCAL, C), bf16),
            pltpu.VMEM((LOCAL, S, C), bf16),
            pltpu.VMEM((LOCAL + 1, S, C), bf16),
            dma, dma((2,)), dma((2,)), dma((2,)), dma, dma((2,)), dma, dma,
        ],
        compiler_params=pltpu.CompilerParams(
            collective_id=0, has_side_effects=True, vmem_limit_bytes=60 * 2**20
        ),
        cost_estimate=pl.CostEstimate(
            flops=34_000_000_000, bytes_accessed=12_000_000, transcendentals=50_000_000
        ),
    )(
        patches, conv_weight, conv_bias.reshape(1, C), norm_gain, row_qkv, row_out, col_qkv, col_out,
        up_weight, down_weight,
    )
    return pl.pallas_call(
        rows_of_columns,
        grid=(N // SOURCES,),
        in_specs=[pl.BlockSpec((SOURCES, LOCAL, LOCAL, C), lambda i: (i, 0, 0, 0))],
        out_specs=pl.BlockSpec((LOCAL, SOURCES * LOCAL, C), lambda i: (0, i, 0)),
        out_shape=jax.ShapeDtypeStruct(patches.shape, bf16),
        scratch_shapes=[pltpu.VMEM((256, 256), bf16)],
        compiler_params=pltpu.CompilerParams(vmem_limit_bytes=60 * 2**20),
        cost_estimate=pl.CostEstimate(flops=1_100_000_000, bytes_accessed=8_400_000, transcendentals=0),
    )(landed)


def solution(mesh):
    return jax.shard_map(
        on_device,
        mesh=mesh,
        in_specs=(P(("batch", "rows"), None, None), P(), P(), P(), P(), P(), P(), P(), P(), P()),
        out_specs=P(("batch", "rows"), None, None),
        check_vma=False,
    )
```

```python
import functools
import math

import jax
import jax.numpy as jnp
from jax import lax
from jax.experimental import pallas as pl
from jax.experimental.pallas import tpu as pltpu
from jax.sharding import PartitionSpec as P

MESH = pl.DeviceIdType.MESH
f32, bf16 = jnp.float32, jnp.bfloat16
HEADS = 8
KS = 7
MARGIN = 3
C = 256
S = 256
N = 8
LOCAL = 32
TILE = 8
SOURCES = 2
GELU_A = math.sqrt(2 / math.pi)
SCALE = math.log2(math.e) / math.sqrt(C // HEADS)

NN = (((1,), (0,)), ((), ()))
NT = (((1,), (1,)), ((), ()))
dot = functools.partial(lax.dot_general, preferred_element_type=f32)


def normalize(x, gain):
    center = x - jnp.mean(x, axis=-1, keepdims=True)
    spread = jnp.mean(center * center, axis=-1, keepdims=True)
    return (center * lax.rsqrt(spread + 1e-5) * gain).astype(bf16)


def heads(query, key_t, value, tick, look=2):
    head_of = lax.broadcasted_iota(jnp.int32, (S, 128), 1) // 32
    zeros = jnp.zeros((32, S), bf16)
    none = jnp.zeros((S, 128), bf16)
    one = jnp.ones((S, 128), bf16)

    def score(h):
        g, i = divmod(h, 4)
        key_h = jnp.concatenate(
            [key_t[32 * h : 32 * h + 32] if j == i else zeros for j in range(4)], axis=0
        )
        return dot(query[:, 128 * g : 128 * g + 128], key_h, NN)

    context = []
    ahead = [score(h) for h in range(look)]
    for g in range(2):
        value_g = value[:, 128 * g : 128 * g + 128]
        total = None
        for i in range(4):
            h = 4 * g + i
            scores = ahead.pop(0)
            if h < HEADS - look:
                ahead.append(score(h + look))
            top = jnp.max(scores, axis=1, keepdims=True)
            probs = jnp.exp2((scores - top).astype(bf16))
            tick(h)
            value_h = jnp.concatenate(
                [jnp.where(head_of == i, value_g, none), jnp.where(head_of == i, one, none)], axis=1
            )
            both = dot(probs, value_h, NN)
            total = both if total is None else total + both
        context.append((total[:, :128] / total[:, 128:]).astype(bf16))
    return jnp.concatenate(context, axis=1)


def gelu(x):
    half = 0.5 * x
    inner = x * (GELU_A + (GELU_A * 0.044715) * (x * x))
    return half + half * jnp.tanh(inner)


def tree_sum(terms):
    while len(terms) > 1:
        odd = [terms[-1]] if len(terms) % 2 else []
        terms = [a + b for a, b in zip(terms[::2], terms[1::2])] + odd
    return terms[0]


def convolve(xin, taps, bias, sums, r, store):
    for t in range(S // TILE + 1):
        if t < S // TILE:
            at = TILE * t
            rows = [xin[r + a, at : at + TILE, :] for a in range(KS)]
            for b in range(KS):
                total = tree_sum([rows[a] * taps[a * KS + b] for a in range(KS)]).astype(f32)
                for half in range(2):
                    sums[half, b, 8 + at : 8 + at + TILE, :] = total[:, 128 * half : 128 * half + 128]
        if t:
            at = TILE * (t - 1)
            y = xin[r + MARGIN, at : at + TILE, :].astype(f32) + bias[...]
            parts = []
            for half in range(2):
                part = y[:, 128 * half : 128 * half + 128]
                for b in range(KS):
                    first = 8 + at + b - MARGIN
                    part = part + sums[half, b, first : first + TILE, :]
                parts.append(part)
            store(at, jnp.concatenate(parts, axis=1).astype(bf16))
        yield


ORDER = {
    0: [("finish", 0)],
    7: [
        ("finish", 1), ("finish", 2), ("norm", 0), ("finish", 3), ("finish", 4),
        ("project", 0), ("project", 1), ("project", 2),
    ],
}


def swap_matrix():
    i0 = lax.broadcasted_iota(jnp.int32, (256, 256), 0)
    i1 = lax.broadcasted_iota(jnp.int32, (256, 256), 1)
    chosen = (i0 // 16 == i1 % 16) & (i0 % 16 == i1 // 16)
    return jnp.where(chosen, jnp.float32(1), jnp.float32(0)).astype(bf16)


def rows_of_columns(landed, out, swap):
    @pl.when(pl.program_id(0) == 0)
    def _():
        swap[...] = swap_matrix()

    for source in range(SOURCES):
        for half in range(2):
            column = source * LOCAL + 16 * half
            for g in range(2):
                block = landed[source, 16 * half : 16 * half + 16, 16 * g : 16 * g + 16, :].reshape(256, C)
                turned = dot(swap[...], block, NN).astype(bf16).reshape(16, 16, C)
                first = 16 * g + MARGIN
                head = min(16, LOCAL - first)
                out[first : first + head, column : column + 16, :] = turned[:head]
                if head < 16:
                    out[0 : 16 - head, column : column + 16, :] = turned[head:]


def kernel(
    x_hbm, conv_w, bias, gains, row_qkv, row_out, col_qkv, col_out, up, down,
    landed,
    xin, taps, sums, query, key_t, value, context, row_kt, col_kt, swap, send1, recv1, cols, send2,
    in_sem, halo_send, halo_recv, own1, send_sem1, recv_sem1, send_sem2, recv_sem2,
):
    me = lax.axis_index("rows")
    last = N - 1

    load = pltpu.make_async_copy(x_hbm, xin.at[pl.ds(MARGIN, LOCAL)], in_sem)
    load.start()

    barrier = pltpu.get_barrier_semaphore()
    for i in range(1, N):
        pl.semaphore_signal(
            barrier, inc=1, device_id={"rows": lax.rem(me + i, N)}, device_id_type=MESH
        )
    def halo(which, target):
        first = LOCAL - MARGIN if which == 0 else 0
        put = 0 if which == 0 else MARGIN + LOCAL
        return pltpu.make_async_remote_copy(
            x_hbm.at[pl.ds(first, MARGIN)],
            xin.at[pl.ds(put, MARGIN)],
            halo_send.at[which],
            halo_recv.at[which],
            device_id={"rows": target},
            device_id_type=MESH,
        )

    @pl.when(me == 0)
    def _():
        xin[0:MARGIN] = jnp.zeros((MARGIN, S, C), bf16)

    @pl.when(me == last)
    def _():
        xin[MARGIN + LOCAL :] = jnp.zeros((MARGIN, S, C), bf16)

    for t in range(KS * KS):
        taps[t] = jnp.broadcast_to(conv_w[t : t + 1, :], (TILE, C)).astype(bf16)
    sums[:, :, 0:8, :] = jnp.zeros((2, KS, 8, 128), f32)
    sums[:, :, 8 + S :, :] = jnp.zeros((2, KS, 8, 128), f32)
    row_kt[...] = row_qkv[:, C : 2 * C].T
    col_kt[...] = col_qkv[:, C : 2 * C].T
    swap[...] = swap_matrix()

    load.wait()

    def project(normed, w_qkv, w_key_t, s, part):
        if part == 0:
            query[s] = (dot(normed, w_qkv[:, :C], NN) * SCALE).astype(bf16)
        if part == 1:
            value[s] = dot(normed, w_qkv[:, 2 * C :], NN).astype(bf16)
        if part == 2:
            key_t[s] = dot(w_key_t[...], normed, NT).astype(bf16)

    def conv_slot(slot):
        def store(at, y):
            send1[slot + 1, at : at + TILE, :] = y

        return convolve(xin, taps, bias, sums, lax.rem(slot + MARGIN, LOCAL), store)

    def send_rows(first, count, early):
        slots = pl.ds(first + 1, count)
        for i in range(1, N):
            to = lax.rem(me + i, N)
            pltpu.make_async_remote_copy(
                send1.at[slots, pl.ds(pl.multiple_of(to * LOCAL, LOCAL), LOCAL)],
                recv1.at[N - i, pl.ds(first, count)],
                send_sem1,
                recv_sem1.at[early],
                device_id={"rows": to},
                device_id_type=MESH,
            ).start()
        pltpu.make_async_copy(
            send1.at[slots, pl.ds(pl.multiple_of(me * LOCAL, LOCAL), LOCAL)],
            recv1.at[0, pl.ds(first, count)],
            own1.at[early],
        ).start()

    def first_conv(slot, _):
        for _ in conv_slot(slot):
            pass
        return 0

    lax.fori_loop(0, 2, first_conv, 0)

    pl.semaphore_wait(barrier, N - 1)

    @pl.when(me < last)
    def _():
        halo(0, lax.rem(me + 1, N)).start()

    @pl.when(me > 0)
    def _():
        halo(1, lax.rem(me + N - 1, N)).start()

    normed = normalize(send1[1].astype(f32), gains[0:1, :])
    for part in range(3):
        project(normed, row_qkv, row_kt, 0, part)
    send1[0] = jnp.zeros((S, C), bf16)
    context[1] = jnp.zeros((S, C), bf16)

    def row_step(j, _):
        @pl.when(j == (LOCAL - 2 * MARGIN) // 2 - 1)
        def _():
            @pl.when(me > 0)
            def _():
                halo(0, me).wait_recv()

            @pl.when(me < last)
            def _():
                halo(1, me).wait_recv()

        for u in range(2):
            t = 2 * j + u
            pieces = conv_slot(t + 2)
            held = {}

            def tick(h, t=t, u=u, pieces=pieces, held=held):
                if h == 0:
                    held["normed"] = normalize(send1[t + 2].astype(f32), gains[0:1, :])
                if h == 2:
                    project(held["normed"], row_qkv, row_kt, 1 - u, 0)
                if h == 4:
                    project(held["normed"], row_qkv, row_kt, 1 - u, 1)
                if h == 5:
                    project(held["normed"], row_qkv, row_kt, 1 - u, 2)
                if h == 6:
                    change = dot(context[1 - u], row_out[...], NN)
                    send1[t] = (send1[t].astype(f32) + change).astype(bf16)

            context[u] = heads(query[u], key_t[u], value[u], tick)
            for _ in pieces:
                pass

        @pl.when(j == 0)
        def _():
            send_rows(0, 1, 0)

        @pl.when(j > 0)
        def _():
            send_rows(2 * j - 1, 2, j // 9)

        return 0

    lax.fori_loop(0, LOCAL // 2, row_step, 0)
    send1[LOCAL] = (send1[LOCAL].astype(f32) + dot(context[1], row_out[...], NN)).astype(bf16)
    send_rows(LOCAL - 1, 1, 1)

    for half in range(2):
        slots = pl.ds(0, 17) if half == 0 else pl.ds(17, LOCAL - 17)
        mine = recv1.at[0, slots]
        pltpu.make_async_copy(mine, mine, own1.at[half]).wait()
        arrived = recv1.at[pl.ds(1, N - 1), slots]
        pltpu.make_async_copy(arrived, arrived, recv_sem1.at[half]).wait()

        def turn(j, _, half=half):
            for g in range(2):
                block = recv1[j, 16 * half : 16 * half + 16, 16 * g : 16 * g + 16, :].reshape(256, C)
                turned = dot(swap[...], block, NN).astype(bf16).reshape(16, 16, C)
                cols[16 * g : 16 * g + 16, pl.ds(pl.multiple_of(j * 32 + 16 * half, 16), 16), :] = turned
            return 0

        lax.fori_loop(0, N, turn, 0)

    def send_cols(first, count):
        columns = pl.ds(first + 1, count)
        for i in range(1, N):
            pltpu.make_async_remote_copy(
                send2.at[columns, pl.ds(LOCAL * i, LOCAL)],
                landed.at[me, pl.ds(first, count)],
                send_sem2,
                recv_sem2,
                device_id={"rows": lax.rem(me + i, N)},
                device_id_type=MESH,
            ).start()
        pltpu.make_async_copy(
            send2.at[columns, pl.ds(0, LOCAL)], landed.at[me, pl.ds(first, count)], recv_sem2
        ).start()

    def finish(held, s, c, part):
        if part == 0:
            delta = dot(context[s], col_out[...], NN).astype(bf16).astype(f32)
            y = (cols[c].astype(f32) + delta).astype(bf16)
            cols[c] = y
            held["inner"] = normalize(y.astype(f32), gains[2:3, :])
            return
        units = slice(256 * (part - 1), 256 * part)
        hidden = gelu(dot(held["inner"], up[:, units], NN)).astype(bf16)
        change = dot(hidden, down[units, :], NN)
        held["total"] = change if part == 1 else held["total"] + change
        if part == 4:
            send2[c + 1] = (cols[c].astype(f32) + held["total"]).astype(bf16)

    normed = normalize(cols[0].astype(f32), gains[1:2, :])
    for part in range(3):
        project(normed, col_qkv, col_kt, 0, part)
    context[1] = jnp.zeros((S, C), bf16)

    def col_step(j, _):
        for u in range(2):
            t = 2 * j + u
            held = {}

            def tick(h, t=t, u=u, held=held):
                before = t - 1 if u else jnp.maximum(t - 1, 0)
                for what, n in ORDER.get(h, ()):
                    if what == "norm":
                        held["normed"] = normalize(
                            cols[jnp.minimum(t + 1, LOCAL - 1)].astype(f32), gains[1:2, :]
                        )
                    if what == "project":
                        project(held["normed"], col_qkv, col_kt, 1 - u, n)
                    if what == "finish":
                        finish(held, 1 - u, before, n)

            context[u] = heads(query[u], key_t[u], value[u], tick, 3)

        @pl.when(j == 0)
        def _():
            send_cols(0, 1)

        @pl.when(j > 0)
        def _():
            send_cols(2 * j - 1, 2)

        return 0

    lax.fori_loop(0, LOCAL // 2, col_step, 0)
    held = {}
    for part in range(5):
        finish(held, 1, LOCAL - 1, part)
    send_cols(LOCAL - 1, 1)

    pltpu.make_async_copy(landed, landed, recv_sem2).wait()
    sent = send1.at[pl.ds(0, LOCAL // N * (N - 1))]
    pltpu.make_async_copy(sent, sent, send_sem1).wait()
    sent = send2.at[pl.ds(0, LOCAL // N * (N - 1))]
    pltpu.make_async_copy(sent, sent, send_sem2).wait()

    @pl.when(me < last)
    def _():
        halo(0, me).wait_send()

    @pl.when(me > 0)
    def _():
        halo(1, me).wait_send()


def on_device(
    patches, conv_weight, conv_bias, norm_gain, row_qkv, row_out, col_qkv, col_out, up_weight, down_weight
):
    vmem = pl.BlockSpec(memory_space=pltpu.VMEM)
    hbm = pl.BlockSpec(memory_space=pl.ANY)
    dma = pltpu.SemaphoreType.DMA
    landed = pl.pallas_call(
        kernel,
        out_shape=jax.ShapeDtypeStruct((N, LOCAL, LOCAL, C), bf16),
        in_specs=[hbm] + [vmem] * 9,
        out_specs=hbm,
        scratch_shapes=[
            pltpu.VMEM((LOCAL + 2 * MARGIN, S, C), bf16),
            pltpu.VMEM((KS * KS, TILE, C), bf16),
            pltpu.VMEM((2, KS, S + 16, 128), f32),
            pltpu.VMEM((2, S, C), bf16),
            pltpu.VMEM((2, C, S), bf16),
            pltpu.VMEM((2, S, C), bf16),
            pltpu.VMEM((2, S, C), bf16),
            pltpu.VMEM((C, C), bf16),
            pltpu.VMEM((C, C), bf16),
            pltpu.VMEM((256, 256), bf16),
            pltpu.VMEM((LOCAL + 3, S, C), bf16),
            pltpu.VMEM((N, LOCAL, LOCAL, C), bf16),
            pltpu.VMEM((LOCAL, S, C), bf16),
            pltpu.VMEM((LOCAL + 1, S, C), bf16),
            dma, dma((2,)), dma((2,)), dma((2,)), dma, dma((2,)), dma, dma,
        ],
        compiler_params=pltpu.CompilerParams(
            collective_id=0, has_side_effects=True, vmem_limit_bytes=60 * 2**20
        ),
        cost_estimate=pl.CostEstimate(
            flops=34_000_000_000, bytes_accessed=12_000_000, transcendentals=50_000_000
        ),
    )(
        patches, conv_weight, conv_bias.reshape(1, C), norm_gain, row_qkv, row_out, col_qkv, col_out,
        up_weight, down_weight,
    )
    return pl.pallas_call(
        rows_of_columns,
        grid=(N // SOURCES,),
        in_specs=[pl.BlockSpec((SOURCES, LOCAL, LOCAL, C), lambda i: (i, 0, 0, 0))],
        out_specs=pl.BlockSpec((LOCAL, SOURCES * LOCAL, C), lambda i: (0, i, 0)),
        out_shape=jax.ShapeDtypeStruct(patches.shape, bf16),
        scratch_shapes=[pltpu.VMEM((256, 256), bf16)],
        compiler_params=pltpu.CompilerParams(vmem_limit_bytes=60 * 2**20),
        cost_estimate=pl.CostEstimate(flops=1_100_000_000, bytes_accessed=8_400_000, transcendentals=0),
    )(landed)


def solution(mesh):
    return jax.shard_map(
        on_device,
        mesh=mesh,
        in_specs=(P(("batch", "rows"), None, None), P(), P(), P(), P(), P(), P(), P(), P(), P()),
        out_specs=P(("batch", "rows"), None, None),
        check_vma=False,
    )
```
